32 devices in a mesh: tensor: 4 (over z), context: 8 (over y, x, core).
Axes of the slice: x: 2, y: 2, z: 4, core: 2. Of those that a mesh axis runs over, the one named last changes fastest.
Arguments:
- query_in: bfloat16 [8192, 4096], P('context', 'tensor'), may hold values from -6 to 6
- key_in: bfloat16 [8192, 4096], P('context', 'tensor'), may hold values from -6 to 6
- value_in: bfloat16 [8192, 4096], P('context', 'tensor'), may hold values from -6 to 6
- filter_taps: bfloat16 [128, 4096], P(None, 'tensor'), may hold values from -0.5 to 0.5
- out_weight: bfloat16 [4096, 4096], P('tensor'), may hold values from -0.09375 to 0.09375
- out_grad: bfloat16 [8192, 4096], P('context', 'tensor'), may hold values from -6 to 6
Outputs:
- grad_query: float32 [8192, 4096], P('context', 'tensor')
- grad_key: float32 [8192, 4096], P('context', 'tensor')
- grad_value: float32 [8192, 4096], P('context', 'tensor')
- grad_filter: float32 [128, 4096], P(None, ('tensor', 'context'))
- grad_weight: float32 [4096, 4096], P('tensor', 'context')
The draws below stay inside these ranges and needn't reach their ends.
All inputs are finite; a program needn't handle non-finite values.
Results may differ from the reference program's by a relative error of at most 0.0045.
Values may be sent and summed in bfloat16 or wider, within the bound.
No kernel may reach another device: no remote copies, remote signals or barrier semaphores. Data moves between devices by JAX's collectives and lax.ppermute only.
A program may use at most 256 MiB of HBM per device.

```python
import jax
import jax.numpy as jnp

D = 4096
FILT = 128
TOKENS = 8192


def with_spikes(entries, rng, source, target, parts, factor):
    def block_of(axis_at):
        return (jnp.arange(entries.shape[axis_at]) // (entries.shape[axis_at] // parts)).reshape((-1,) + (1,) * (entries.ndim - 1 - axis_at))

    near = jax.random.permutation(rng, parts)[block_of(target)]
    far = (block_of(target) + parts // 2) % parts
    return jnp.where((block_of(source) == near) | (block_of(source) == far), factor * entries, entries)


def levels(rng, dims, pieces, smallest, high):
    level, own = 1.0, jax.random.fold_in(rng, 6)
    for dim, blocks in pieces:
        heights = jnp.exp(jax.random.uniform(jax.random.fold_in(own, dim), (blocks,), jnp.float32, smallest / len(pieces), high / len(pieces)))
        level = level * jnp.repeat(heights, dims[dim] // blocks).reshape([-1 if axis == dim else 1 for axis in range(len(dims))])
    return level


def normal_values(stream_key, extent, width, bound, pieces=(), kind=jnp.bfloat16):
    array = jax.random.normal(stream_key, extent, jnp.float32) * width
    if len(pieces) > 0:
        array = levels(stream_key, extent, pieces, -0.22, 0.18) * array
    return jnp.clip(array, min=-bound, max=bound).astype(kind)


def bell_draw_with(rng, shape, spread, reach, cuts, heavy, dtype=jnp.bfloat16):
    drawn = spread * jax.random.normal(rng, shape, jnp.float32)
    if cuts:
        drawn = drawn * levels(rng, shape, cuts, -0.22, 0.18)
    return jnp.clip(with_spikes(drawn, jax.random.fold_in(rng, 3), *heavy), -reach, reach).astype(dtype)


def setup_inputs(seed: int = 0) -> dict:
    seeds = jax.random.split(jax.random.key(seed), 7)
    return {
        "query_in": normal_values(seeds[0], (TOKENS, D), 1.0, 6.0, ((0, 8), (1, 4))),
        "key_in": normal_values(seeds[1], (TOKENS, D), 1.0, 6.0, ((0, 8), (1, 4))),
        "value_in": normal_values(seeds[2], (TOKENS, D), 1.0, 6.0, ((0, 8), (1, 4))),
        "filter_taps": normal_values(seeds[3], (FILT, D), FILT ** -0.5, 0.5, ((1, 4),)),
        "out_weight": normal_values(seeds[4], (D, D), D ** -0.5, 0.09375, ((0, 4),)),
        "out_grad": bell_draw_with(seeds[5], (TOKENS, D), 1.0, 6.0, ((0, 8), (1, 4)), (0, 1, 8, 2.0)),
    }


def reference(query_in, key_in, value_in, filter_taps, out_weight, out_grad):
    length = TOKENS * 2
    mixed_in = (key_in.astype(jnp.float32) * value_in.astype(jnp.float32)).astype(jnp.bfloat16)
    mixed_freq = jnp.fft.rfft(mixed_in.astype(jnp.float32), length, axis=0)
    taps_freq = jnp.fft.rfft(filter_taps.astype(jnp.float32), length, axis=0)
    conv_out = jnp.fft.irfft(mixed_freq * taps_freq, length, axis=0)[:TOKENS].astype(jnp.float32)
    gated = (query_in.astype(jnp.float32) * conv_out).astype(jnp.bfloat16)
    grad_gated = jnp.dot(out_grad, out_weight.T, preferred_element_type=jnp.float32)
    grad_query = (grad_gated * conv_out).astype(jnp.float32)
    grad_conv = (grad_gated * query_in.astype(jnp.float32)).astype(jnp.bfloat16)
    conv_freq = jnp.fft.rfft(grad_conv.astype(jnp.float32), length, axis=0)
    grad_mixed = jnp.fft.irfft(conv_freq * jnp.conj(taps_freq), length, axis=0)[:TOKENS].astype(jnp.float32)
    grad_key = (grad_mixed * value_in.astype(jnp.float32)).astype(jnp.float32)
    grad_value = (grad_mixed * key_in.astype(jnp.float32)).astype(jnp.float32)
    loss_scale = TOKENS ** -0.5
    grad_filter = jnp.fft.irfft(conv_freq * jnp.conj(mixed_freq), length, axis=0)[:FILT].astype(jnp.float32) * loss_scale
    grad_weight = jnp.dot(gated.T, out_grad, preferred_element_type=jnp.float32) * loss_scale
    return grad_query, grad_key, grad_value, grad_filter, grad_weight
```

```python
import functools
import math

import jax
import jax.numpy as jnp
import numpy as np
from jax import lax
from jax.experimental import pallas as pl
from jax.experimental.pallas import tpu as pltpu
from jax.sharding import PartitionSpec as P

BF16 = jnp.bfloat16
F32 = jnp.float32
VMEM_LIMIT = 48 * 1024 * 1024

ANYWHERE = pl.BlockSpec(memory_space=pl.ANY)
SCALAR = pl.BlockSpec(memory_space=pltpu.SMEM)


def weight_of(micros):
    return pl.CostEstimate(flops=1 << 20, bytes_accessed=int(micros * 3.7e6), transcendentals=0)


def split_const(matrix):
    high = matrix.astype(np.float32).astype(jnp.bfloat16)
    low = (matrix - high.astype(np.float64)).astype(np.float32).astype(jnp.bfloat16)
    return high, low


def odd_dft(span):
    freq = np.pi * (np.arange(span) + 0.5) / span
    pos = np.arange(span)
    ahead = np.outer(freq, pos)
    forward = np.concatenate([np.cos(ahead), -np.sin(ahead)], axis=0)

    def backward(at):
        angle = np.outer(at, freq)
        return np.concatenate([np.cos(angle), -np.sin(angle)], axis=1) / span

    f_high, f_low = split_const(forward)
    stacks = []
    for at in (span + pos, pos, span - pos):
        b_high, b_low = split_const(backward(at))
        stacks.append(np.concatenate([b_high, b_low], axis=0))
    return np.concatenate([f_high, f_low], axis=1), stacks


def dot(lhs, rhs):
    return jnp.dot(lhs, rhs, preferred_element_type=F32)


def to_freq(fwd, block):
    return dot(fwd, jnp.concatenate([block, block], axis=0))


def from_freq(stack, value, passes):
    span = stack.shape[0] // 2
    high = value.astype(BF16)
    if passes == 1:
        return dot(stack[:span], high)
    both = dot(stack, high)
    total = both[:span] + both[span:]
    if passes == 3:
        total = total + dot(stack[:span], (value - high.astype(F32)).astype(BF16))
    return total


def signs(span):
    row = lax.broadcasted_iota(jnp.int32, (span, 1), 0)
    return jnp.where(lax.rem(row, 2) == 0, 1.0, -1.0).astype(F32)


def window(first, second, sign):
    span = sign.shape[0]
    real = first[:span] + sign * second[span:]
    imag = first[span:] - sign * second[:span]
    return real, imag


def conv_kernel(start_ref, q_ref, k_ref, v_ref, halo_ref, taps_ref, fwd_ref, inv_ref, conv_ref, gated_ref):
    span = taps_ref.shape[0]
    sign = signs(span)
    taps = to_freq(fwd_ref[...], taps_ref[...])
    tr, ti = taps[:span], taps[span:]
    halo = jnp.where(start_ref[0] == 1, jnp.zeros_like(halo_ref), halo_ref[...])
    prev = to_freq(fwd_ref[...], halo)
    for b in range(q_ref.shape[0] // span):
        rows = pl.ds(b * span, span)
        mixed = (k_ref[rows, :].astype(F32) * v_ref[rows, :].astype(F32)).astype(BF16)
        cur = to_freq(fwd_ref[...], mixed)
        xr, xi = window(prev, cur, sign)
        spec = jnp.concatenate([xr * tr - xi * ti, xr * ti + xi * tr], axis=0)
        conv = from_freq(inv_ref[...], spec, 3)
        conv_ref[rows, :] = conv.astype(BF16)
        gated_ref[:, rows] = jnp.transpose(q_ref[rows, :].astype(F32) * conv).astype(BF16)
        prev = cur


def filtered(is_start, query, key, value, halo, taps, consts):
    rows, chans = query.shape
    span = taps.shape[0]
    tile = min(256, chans)
    fwd, stacks = consts
    col = pl.BlockSpec((rows, tile), lambda i: (0, i))
    short = pl.BlockSpec((span, tile), lambda i: (0, i))
    whole = pl.BlockSpec((2 * span, 2 * span), lambda i: (0, 0))
    return pl.pallas_call(
        conv_kernel,
        grid=(chans // tile,),
        in_specs=[SCALAR, col, col, col, short, short, whole, whole],
        out_specs=[
            col,
            pl.BlockSpec((tile, rows), lambda i: (i, 0)),
        ],
        out_shape=[
            jax.ShapeDtypeStruct((rows, chans), BF16),
            jax.ShapeDtypeStruct((chans, rows), BF16),
        ],
        compiler_params=pltpu.CompilerParams(vmem_limit_bytes=VMEM_LIMIT),
        cost_estimate=weight_of(100),
        name="filtered",
    )(is_start, query, key, value, halo, taps, fwd, stacks[0])


def pair_dot(lhs, rhs):
    return lax.dot_general(lhs, rhs, (((1,), (1,)), ((), ())), preferred_element_type=F32)


def read_pick(refs, second):
    value = refs[0][...]
    for ref in refs[1:]:
        value = jnp.where(second, ref[...], value)
    return value


class Operands:
    def __init__(self, slots, weight, tile, wide, weighted):
        rows = slots[0][1][0][0].shape[0]
        per_core = weight.shape[0] // (2 * wide)
        self.arrays, self.specs, self.groups, self.weights = [], [], [], []
        for held, parts, offset in slots:
            for side in range(2):
                group = []
                for array, at in parts:
                    column = at + side * (array.shape[1] // (2 * wide))
                    group.append(len(self.arrays))
                    self.arrays.append(array)
                    self.specs.append(pl.BlockSpec((rows, wide), functools.partial(self.fixed, column)))
                self.groups.append(group)
        for held, parts, offset in slots:
            for side in range(2):
                if held not in weighted:
                    self.weights.append(None)
                    continue
                at = side * per_core + offset // wide
                self.weights.append(len(self.arrays))
                self.arrays.append(weight)
                self.specs.append(
                    pl.BlockSpec((tile, wide), functools.partial(self.placed, held, 2 * per_core, at))
                )

    @staticmethod
    def fixed(column, i, place):
        return (0, column)

    @staticmethod
    def placed(held, blocks, at, i, place):
        return (i, place[held] * blocks + at)

    def values(self, refs, place_ref):
        second = place_ref[7] == 1
        sides = [read_pick([refs[n] for n in group], second) for group in self.groups]
        return [jnp.concatenate(sides[n : n + 2], axis=1) for n in range(0, len(sides), 2)]

    def weight_values(self, refs):
        sides = [None if n is None else refs[n][...] for n in self.weights]
        return [
            None if sides[n] is None else jnp.concatenate(sides[n : n + 2], axis=1)
            for n in range(0, len(sides), 2)
        ]


def project_kernel(place_ref, *refs, operands, products, earlier, carried):
    count = len(operands.arrays)
    blocks, rest = refs[:count], list(refs[count + earlier :])
    values = operands.values(blocks, place_ref)
    if "outer" in products:
        gated_ref = rest.pop(0)
        outs = [rest.pop() for _ in range(2 * len(values))][::-1]
        first_core = place_ref[4] == 0
        wide = outs[0].shape[1]
        outers = [dot(gated_ref[...], value).astype(BF16) for value in values]
        if len(outers) == 2:
            first_keeps = place_ref[5] == 0
            outers = [
                jnp.where(first_keeps, outers[0], outers[1]),
                jnp.where(first_keeps, outers[1], outers[0]),
            ]
        for n, outer in enumerate(outers):
            left, right = outer[:, :wide], outer[:, wide:]
            outs[2 * n][...] = jnp.where(first_core, left, right)
            outs[2 * n + 1][...] = jnp.where(first_core, right, left)
    if "inner" in products:
        total = rest.pop(0)[...] if carried else None
        for value, weight in zip(values, operands.weight_values(blocks)):
            if weight is not None:
                part = pair_dot(value, weight)
                total = part if total is None else total + part
        rest[0][...] = total


def project(place, slots, gated_t, weight, acc, wide, products, earlier, weighted, micros=100):
    chans, rows = gated_t.shape
    tile = min(256 if "inner" in products else 512, chans)
    operands = Operands(slots, weight, tile, wide, weighted)
    col = pl.BlockSpec((rows, tile), lambda i, p: (0, i))
    carried = "inner" in products and acc is not None
    outs, out_specs, specs, arrays = [], [], [], []
    if "outer" in products:
        specs.append(pl.BlockSpec((tile, rows), lambda i, p: (i, 0)))
        arrays.append(gated_t)
    if "inner" in products:
        outs.append(jax.ShapeDtypeStruct((rows, chans), F32))
        out_specs.append(col)
        if carried:
            specs.append(col)
            arrays.append(acc)
    if "outer" in products:
        outs += [jax.ShapeDtypeStruct((chans, wide), BF16)] * (2 * len(slots))
        out_specs += [pl.BlockSpec((tile, wide), lambda i, p: (i, 0))] * (2 * len(slots))
    return pl.pallas_call(
        functools.partial(
            project_kernel, operands=operands, products=products, earlier=len(earlier), carried=carried
        ),
        grid_spec=pltpu.PrefetchScalarGridSpec(
            num_scalar_prefetch=1,
            grid=(chans // tile,),
            in_specs=operands.specs + [ANYWHERE] * len(earlier) + specs,
            out_specs=out_specs,
        ),
        out_shape=outs,
        compiler_params=pltpu.CompilerParams(vmem_limit_bytes=VMEM_LIMIT),
        cost_estimate=weight_of(micros),
        name="project",
    )(place, *operands.arrays, *earlier, *arrays)


def grad_kernel(place_ref, *refs, operands, earlier, scale):
    count = len(operands.arrays) if operands else 0
    blocks = refs[:count]
    count += earlier
    acc_ref, conv_ref, q_ref, k_ref, v_ref, start_ref, before_ref, taps_ref, fwd_ref, inv_ref, lag_ref = refs[
        count : count + 11
    ]
    gq_ref, gk_ref, gv_ref, first_ref, last_ref, gf_ref = refs[count + 11 :]
    span, chans = taps_ref.shape
    sign = signs(span)
    taps = to_freq(fwd_ref[...], taps_ref[...])
    tr, ti = taps[:span], taps[span:]
    acc_r = jnp.zeros((span, chans), F32)
    acc_i = jnp.zeros((span, chans), F32)
    if operands:
        value = jnp.concatenate(operands.values(blocks, place_ref), axis=1)
        weight = jnp.concatenate(operands.weight_values(blocks), axis=1)
        added = pair_dot(value, weight)
    last = q_ref.shape[0] // span - 1
    halo = jnp.where(start_ref[0] == 1, jnp.zeros_like(before_ref), before_ref[...])
    prev_mixed = to_freq(fwd_ref[...], halo)
    prev = None
    for b in range(last + 1):
        rows = pl.ds(b * span, span)
        gg = acc_ref[rows, :]
        if operands:
            gg = gg + added[b * span : (b + 1) * span]
        gq_ref[rows, :] = gg * conv_ref[rows, :].astype(F32)
        grad_conv = (gg * q_ref[rows, :].astype(F32)).astype(BF16)
        if b == 0:
            first_ref[...] = grad_conv
        if b == last:
            last_ref[...] = grad_conv
        grad = to_freq(fwd_ref[...], grad_conv)
        mixed = (k_ref[rows, :].astype(F32) * v_ref[rows, :].astype(F32)).astype(BF16)
        cur = to_freq(fwd_ref[...], mixed)
        xr, xi = window(prev_mixed, cur, sign)
        prev_mixed = cur
        gr, gi = grad[:span], grad[span:]
        acc_r += gr * xr + gi * xi
        acc_i += gr * xi - gi * xr
        if b > 0:
            rows = pl.ds((b - 1) * span, span)
            back = filtered_back(prev, grad, tr, ti, sign, inv_ref[...])
            gk_ref[rows, :] = back * v_ref[rows, :].astype(F32)
            gv_ref[rows, :] = back * k_ref[rows, :].astype(F32)
        prev = grad
    part = from_freq(lag_ref[...], jnp.concatenate([acc_r, acc_i], axis=0), 3) * scale
    wide = gf_ref.shape[2]
    for n in range(gf_ref.shape[0]):
        gf_ref[n] = part[:, n * wide : (n + 1) * wide]


def filtered_back(cur, later, tr, ti, sign, stack):
    wr, wi = window(cur, later, sign)
    return from_freq(stack, jnp.concatenate([wr * tr + wi * ti, wi * tr - wr * ti], axis=0), 2)


def gradients(
    place, slots, weight, wide, acc, conv, query, key, value, is_start, before, taps, consts, contexts, scale, earlier
):
    rows, chans = query.shape
    span = taps.shape[0]
    tile = min(256, chans)
    own = chans // contexts
    fwd, stacks = consts
    operands = Operands(slots, weight, tile, wide, [held for held, _, _ in slots]) if slots else None
    col = pl.BlockSpec((rows, tile), lambda i, p: (0, i))
    short = pl.BlockSpec((span, tile), lambda i, p: (0, i))
    whole = pl.BlockSpec((2 * span, 2 * span), lambda i, p: (0, 0))
    return pl.pallas_call(
        functools.partial(grad_kernel, operands=operands, earlier=len(earlier), scale=scale),
        grid_spec=pltpu.PrefetchScalarGridSpec(
            num_scalar_prefetch=1,
            grid=(chans // tile,),
            in_specs=(operands.specs if slots else [])
            + [ANYWHERE] * len(earlier)
            + [col, col, col, col, col, SCALAR, short, short, whole, whole, whole],
            out_specs=[
                col,
                col,
                col,
                short,
                short,
                pl.BlockSpec((tile // own, span, own), lambda i, p: (i, 0, 0)),
            ],
        ),
        out_shape=[jax.ShapeDtypeStruct((rows, chans), F32)] * 3
        + [
            jax.ShapeDtypeStruct((span, chans), BF16),
            jax.ShapeDtypeStruct((span, chans), BF16),
            jax.ShapeDtypeStruct((contexts, span, own), F32),
        ],
        compiler_params=pltpu.CompilerParams(vmem_limit_bytes=VMEM_LIMIT),
        cost_estimate=weight_of(100),
        name="gradients",
    )(
        place, *(operands.arrays if slots else []), *earlier,
        acc, conv, query, key, value, is_start, before, taps, fwd, stacks[1], stacks[2],
    )


def last_kernel(end_ref, last_ref, after_ref, k_ref, v_ref, taps_ref, fwd_ref, inv_ref, gk_in, gv_in, gk_ref, gv_ref):
    span = taps_ref.shape[0]
    taps = to_freq(fwd_ref[...], taps_ref[...])
    cur = to_freq(fwd_ref[...], last_ref[...])
    later = to_freq(fwd_ref[...], jnp.where(end_ref[0] == 1, jnp.zeros_like(after_ref), after_ref[...]))
    back = filtered_back(cur, later, taps[:span], taps[span:], signs(span), inv_ref[...])
    gk_ref[...] = back * v_ref[...].astype(F32)
    gv_ref[...] = back * k_ref[...].astype(F32)


def last_rows(is_end, last, after_rows, key, value, taps, grad_key, grad_value, consts):
    rows, chans = key.shape
    span = taps.shape[0]
    tile = min(512, chans)
    fwd, stacks = consts
    bottom = rows // span - 1
    low = pl.BlockSpec((span, tile), lambda i: (bottom, i))
    short = pl.BlockSpec((span, tile), lambda i: (0, i))
    whole = pl.BlockSpec((2 * span, 2 * span), lambda i: (0, 0))
    return pl.pallas_call(
        last_kernel,
        grid=(chans // tile,),
        in_specs=[
            SCALAR, short, short, low, low, short, whole, whole, ANYWHERE, ANYWHERE,
        ],
        out_specs=[low, low],
        out_shape=[jax.ShapeDtypeStruct((rows, chans), F32)] * 2,
        input_output_aliases={8: 0, 9: 1},
        compiler_params=pltpu.CompilerParams(vmem_limit_bytes=VMEM_LIMIT),
        cost_estimate=weight_of(2),
        name="last_rows",
    )(is_end, last, after_rows, key, value, taps, fwd, stacks[1], grad_key, grad_value)


def finish_kernel(early_ref, *refs, own, groups, across, scale):
    out = refs[-1]
    for cols, late in group_sums(refs[own:], groups, across):
        early = sum(ref[:, cols].astype(F32) for ref in refs[:own])
        out[:, cols] = jnp.where(early_ref[0] == 1, early, late) * scale


def finish(is_early, own_terms, groups, across, out, at, scale):
    rows, wide = across[0].shape
    tile = rows // 2
    terms = [term for group in groups for term in group] + list(across)
    sizes = [(len(group), group[0].shape[1]) for group in groups]
    block = pl.BlockSpec((tile, wide), lambda i, p: (i, at))
    held = [] if out is None else [out]
    return pl.pallas_call(
        functools.partial(finish_kernel, own=len(own_terms), groups=sizes, across=len(across), scale=scale),
        grid_spec=pltpu.PrefetchScalarGridSpec(
            num_scalar_prefetch=1,
            grid=(rows // tile,),
            in_specs=[block] * len(own_terms)
            + [pl.BlockSpec((tile, term.shape[1]), lambda i, p: (i, 0)) for term in terms]
            + [ANYWHERE] * len(held),
            out_specs=block,
        ),
        out_shape=jax.ShapeDtypeStruct((rows, own_terms[0].shape[1]), F32),
        input_output_aliases={1 + len(own_terms) + len(terms): 0} if held else {},
        compiler_params=pltpu.CompilerParams(vmem_limit_bytes=VMEM_LIMIT),
        cost_estimate=weight_of(2),
        name="finish",
    )(is_early, *own_terms, *terms, *held)


def on_line(pairs, contexts):
    return [(a * contexts + c, b * contexts + c) for a, b in pairs for c in range(contexts)]


def send_line(value, pairs, contexts):
    return lax.ppermute(value, ("tensor", "context"), on_line(pairs, contexts))


def swap(value, bit, contexts):
    return lax.ppermute(value, "context", [(c, c ^ bit) for c in range(contexts)])


def pieces_kernel(*refs, pieces):
    outs = refs[-len(pieces) :]
    half = refs[0].shape[1] // 2
    for (offset, wide), out in zip(pieces, outs):
        for side in range(2):
            at = side * half + offset
            out[:, side * wide : (side + 1) * wide] = refs[0][:, at : at + wide]


def cut(block, pieces, earlier):
    rows, chans = block.shape
    return pl.pallas_call(
        functools.partial(pieces_kernel, pieces=pieces),
        grid=(4,),
        in_specs=[pl.BlockSpec((rows // 4, chans), lambda i: (i, 0))] + [ANYWHERE] * len(earlier),
        out_specs=[pl.BlockSpec((rows // 4, 2 * wide), lambda i: (i, 0)) for _, wide in pieces],
        out_shape=[jax.ShapeDtypeStruct((rows, 2 * wide), BF16) for _, wide in pieces],
        cost_estimate=weight_of(100),
        name="cut",
    )(block, *earlier)


def hold_kernel(*refs):
    pass


def hold(value, earlier):
    return pl.pallas_call(
        hold_kernel,
        in_specs=[ANYWHERE] * (1 + len(earlier)),
        out_specs=ANYWHERE,
        out_shape=jax.ShapeDtypeStruct(value.shape, value.dtype),
        input_output_aliases={0: 0},
        cost_estimate=weight_of(1),
        name="hold",
    )(value, *earlier)


def group_sums(refs, groups, across):
    at, column, wide_refs = 0, 0, refs[sum(count for count, _ in groups) :][:across]
    for count, wide in groups:
        cols = slice(column, column + wide)
        terms = [ref[...] for ref in refs[at : at + count]] + [ref[:, cols] for ref in wide_refs]
        yield cols, sum(term.astype(F32) for term in terms)
        at, column = at + count, column + wide


def add_kernel(*refs, groups, across):
    for cols, total in group_sums(refs, groups, across):
        refs[-1][:, cols] = total.astype(BF16)


def add_blocks(groups, earlier, micros=1, across=()):
    rows = groups[0][0].shape[0]
    tile = rows // 2
    terms = [term for group in groups for term in group] + list(across)
    sizes = [(len(group), group[0].shape[1]) for group in groups]
    wide = sum(size for _, size in sizes)
    return pl.pallas_call(
        functools.partial(add_kernel, groups=sizes, across=len(across)),
        grid=(rows // tile,),
        in_specs=[pl.BlockSpec((tile, term.shape[1]), lambda i: (i, 0)) for term in terms]
        + [ANYWHERE] * len(earlier),
        out_specs=pl.BlockSpec((tile, wide), lambda i: (i, 0)),
        out_shape=jax.ShapeDtypeStruct((rows, wide), BF16),
        compiler_params=pltpu.CompilerParams(vmem_limit_bytes=VMEM_LIMIT),
        cost_estimate=weight_of(micros),
        name="add_blocks",
    )(*terms, *earlier)


def body(query, key, value, taps, weight, out_grad, tensors, contexts):
    rows, chans = query.shape
    span = taps.shape[0]
    scale = 1.0 / math.sqrt(rows * contexts)
    consts = odd_dft(span)
    ctx = lax.axis_index("context")
    ten = lax.axis_index("tensor")

    tail = lambda x: x[rows - span :].astype(F32)
    last_mixed = (tail(key) * tail(value)).astype(BF16)
    before = lax.ppermute(last_mixed, "context", [(c, (c + 1) % contexts) for c in range(contexts)])
    is_start = (ctx == 0).astype(jnp.int32).reshape(1)
    is_end = (ctx == contexts - 1).astype(jnp.int32).reshape(1)

    if tensors == 4 and contexts == 8 and chans % 1024 == 0:
        half = chans // 2
        pieces = [(0, half // 2), (half // 2, half // 4), (3 * half // 4, half // 4)]
        chip, core = ctx // 2, lax.rem(ctx, 2)
        low = ten < 2
        edge = (ten == 0) | (ten == 3)
        held = [ten, ten ^ 1, jnp.where(low, 2, 1), jnp.where(low, 3, 0)]
        sides = [(h ^ chip) & 1 for h in held]
        early = jnp.stack(held + [core] + sides[:2] + [edge]).astype(jnp.int32)
        late = jnp.stack(held + [core] + sides[2:] + [edge]).astype(jnp.int32)
        is_early = ((chip // 2) == (ten // 2)).astype(jnp.int32).reshape(1)

        swap_ends = [(0, 1), (1, 0), (2, 3), (3, 2)]
        swap_mid = [(1, 2), (2, 1)]
        over = lambda value, bit: swap(value, bit, contexts)
        pair = send_line(out_grad, swap_ends, contexts)
        near_mid = send_line(out_grad, swap_mid, contexts)
        conv, gated_t = filtered(is_start, query, key, value, before, taps, consts)
        near_end = send_line(near_mid, swap_ends, contexts)

        slots = [(0, [(out_grad, 0)], 0), (1, [(pair, 0)], 0)]
        gg, keep, other_keep, cross, other_cross = project(
            early, slots, gated_t, weight, None, half, ("outer", "inner"), [near_mid], [0, 1]
        )
        far_mid = [send_line(block, swap_mid, contexts) for block in cut(pair, pieces, [gg])]
        far_end = [send_line(block, swap_ends, contexts) for block in far_mid]
        cross_in = add_blocks([[cross, over(other_cross, 1)]], [])
        own_terms = [keep, over(other_keep, 1), over(cross_in, 2)]

        slots = [(2, [(near_mid, 0), (near_end, 0)], 0)]
        (gg,) = project(late, slots, gated_t, weight, gg, half, ("inner",), [cross_in], [2])
        own_in = add_blocks([own_terms], [gg])
        own_terms.append(over(own_in, 4))

        keeps, crosses = [], []
        for n, (offset, wide) in enumerate(pieces):
            slots = [
                (2, [(near_mid, offset // wide), (near_end, offset // wide)], offset),
                (3, [(far_mid[n], 0), (far_end[n], 0)], offset),
            ]
            if n == 0:
                gg, *outer = project(
                    late, slots, gated_t, weight, gg, wide, ("outer", "inner"), [own_in], [3]
                )
            else:
                earlier = [] if n == 1 else [gg, own_terms[-1]]
                outer = project(late, slots, gated_t, weight, None, wide, ("outer",), earlier, [])
            keep, other_keep, cross, other_cross = outer
            keeps.append([keep, over(other_keep, 1)])
            crosses.append([cross, over(other_cross, 1)])
            if n == 1:
                first_cross = add_blocks([crosses[0]], [keep], 0.1)
                keeps[0].append(over(first_cross, 2))
                (gg,) = project(
                    late, slots[1:], gated_t, weight, gg, wide, ("inner",), [first_cross], [3], 0.1
                )
        first_in = add_blocks([keeps[0]], [])
        last_cross = add_blocks(crosses[1:], [first_in])
        last_over = over(last_cross, 2)
        grad_query, grad_key, grad_value, first, last, parts = gradients(
            late, slots[1:], weight, wide, gg, conv, query, key, value, is_start, before, taps, consts,
            contexts, scale, [last_cross],
        )
        first_over = over(first_in, 4)
        grad_weight = finish(is_early, own_terms, keeps[:1], [first_over], None, 0, scale)
        last_in = add_blocks(keeps[1:], [first], 1, [last_over])
        grad_weight = finish(
            is_early, own_terms, keeps[1:], [last_over, over(last_in, 4)], grad_weight, 1, scale
        )
    else:
        conv, gated_t = filtered(is_start, query, key, value, before, taps, consts)
        segment = lax.all_gather(out_grad, "tensor", axis=1, tiled=True)
        gg = lax.dot_general(segment, weight, (((1,), (1,)), ((), ())), preferred_element_type=F32)
        outer = dot(gated_t, segment)
        grad_weight = lax.psum_scatter(outer, "context", scatter_dimension=1, tiled=True) * scale
        grad_query, grad_key, grad_value, first, last, parts = gradients(
            jnp.zeros((1,), jnp.int32), None, weight, 0, gg, conv, query, key, value, is_start, before, taps, consts,
            contexts, scale, [],
        )

    after_rows = lax.ppermute(first, "context", [(c, (c - 1) % contexts) for c in range(contexts)])
    parts = hold(parts, [after_rows])
    parts = lax.all_to_all(parts, "context", split_axis=0, concat_axis=0, tiled=True)
    grad_filter = jnp.sum(parts, axis=0)
    grad_key, grad_value = last_rows(
        is_end, last, after_rows, key, value, taps, grad_key, grad_value, consts
    )
    return (grad_query, grad_key, grad_value, grad_filter, grad_weight)


def solution(mesh):
    placed = (
        P("context", "tensor"),
        P("context", "tensor"),
        P("context", "tensor"),
        P(None, "tensor"),
        P("tensor", None),
        P("context", "tensor"),
    )
    run = functools.partial(body, tensors=mesh.shape["tensor"], contexts=mesh.shape["context"])
    return jax.shard_map(
        run,
        mesh=mesh,
        in_specs=placed,
        out_specs=(
            P("context", "tensor"),
            P("context", "tensor"),
            P("context", "tensor"),
            P(None, ("tensor", "context")),
            P("tensor", "context"),
        ),
        check_vma=False,
    )
```

```python
import functools
import math

import jax
import jax.numpy as jnp
import numpy as np
from jax import lax
from jax.experimental import pallas as pl
from jax.experimental.pallas import tpu as pltpu
from jax.sharding import PartitionSpec as P

BF16 = jnp.bfloat16
F32 = jnp.float32
VMEM_LIMIT = 48 * 1024 * 1024

ANYWHERE = pl.BlockSpec(memory_space=pl.ANY)
SCALAR = pl.BlockSpec(memory_space=pltpu.SMEM)


def weight_of(micros):
    return pl.CostEstimate(flops=1 << 20, bytes_accessed=int(micros * 3.7e6), transcendentals=0)


def split_const(matrix):
    high = matrix.astype(np.float32).astype(jnp.bfloat16)
    low = (matrix - high.astype(np.float64)).astype(np.float32).astype(jnp.bfloat16)
    return high, low


def odd_dft(span):
    freq = np.pi * (np.arange(span) + 0.5) / span * (1 - 2 * (np.arange(span) % 2))
    pos = np.arange(span)
    ahead = np.outer(freq, pos)
    forward = np.concatenate([np.cos(ahead), -np.sin(ahead)], axis=0)

    def backward(at):
        angle = np.outer(at, freq)
        return np.concatenate([np.cos(angle), -np.sin(angle)], axis=1) / span

    f_high, f_low = split_const(forward)
    stacks = []
    for at in (span + pos, pos, span - pos):
        b_high, b_low = split_const(backward(at))
        stacks.append(np.concatenate([b_high, b_low], axis=0))
    return np.concatenate([f_high, f_low], axis=1), stacks


def dot(lhs, rhs):
    return jnp.dot(lhs, rhs, preferred_element_type=F32)


def to_freq(fwd, block):
    return dot(fwd, jnp.concatenate([block, block], axis=0))


def from_freq(stack, value, passes):
    span = stack.shape[0] // 2
    high = value.astype(BF16)
    if passes == 1:
        return dot(stack[:span], high)
    both = dot(stack, high)
    total = both[:span] + both[span:]
    if passes == 3:
        total = total + dot(stack[:span], (value - high.astype(F32)).astype(BF16))
    return total


def window(first, second):
    span = first.shape[0] // 2
    real = first[:span] + second[span:]
    imag = first[span:] - second[:span]
    return real, imag


def conv_kernel(start_ref, q_ref, k_ref, v_ref, halo_ref, taps_ref, fwd_ref, inv_ref, conv_ref, gated_ref):
    span = taps_ref.shape[0]
    taps = to_freq(fwd_ref[...], taps_ref[...])
    tr, ti = taps[:span], taps[span:]
    halo = jnp.where(start_ref[0] == 1, jnp.zeros_like(halo_ref), halo_ref[...])
    prev = to_freq(fwd_ref[...], halo)
    for b in range(q_ref.shape[0] // span):
        rows = pl.ds(b * span, span)
        mixed = (k_ref[rows, :].astype(F32) * v_ref[rows, :].astype(F32)).astype(BF16)
        cur = to_freq(fwd_ref[...], mixed)
        xr, xi = window(prev, cur)
        spec = jnp.concatenate([xr * tr - xi * ti, xr * ti + xi * tr], axis=0)
        conv = from_freq(inv_ref[...], spec, 3)
        conv_ref[rows, :] = conv.astype(BF16)
        gated_ref[:, rows] = jnp.transpose(q_ref[rows, :].astype(F32) * conv).astype(BF16)
        prev = cur


def filtered(is_start, query, key, value, halo, taps, consts):
    rows, chans = query.shape
    span = taps.shape[0]
    tile = min(256, chans)
    fwd, stacks = consts
    col = pl.BlockSpec((rows, tile), lambda i: (0, i))
    short = pl.BlockSpec((span, tile), lambda i: (0, i))
    whole = pl.BlockSpec((2 * span, 2 * span), lambda i: (0, 0))
    return pl.pallas_call(
        conv_kernel,
        grid=(chans // tile,),
        in_specs=[SCALAR, col, col, col, short, short, whole, whole],
        out_specs=[
            col,
            pl.BlockSpec((tile, rows), lambda i: (i, 0)),
        ],
        out_shape=[
            jax.ShapeDtypeStruct((rows, chans), BF16),
            jax.ShapeDtypeStruct((chans, rows), BF16),
        ],
        compiler_params=pltpu.CompilerParams(vmem_limit_bytes=VMEM_LIMIT),
        cost_estimate=weight_of(100),
        name="filtered",
    )(is_start, query, key, value, halo, taps, fwd, stacks[0])


def pair_dot(lhs, rhs):
    return lax.dot_general(lhs, rhs, (((1,), (1,)), ((), ())), preferred_element_type=F32)


def read_pick(refs, second):
    value = refs[0][...]
    for ref in refs[1:]:
        value = jnp.where(second, ref[...], value)
    return value


class Operands:
    def __init__(self, slots, weight, tile, wide, weighted):
        rows = slots[0][1][0][0].shape[0]
        per_core = weight.shape[0] // (2 * wide)
        self.arrays, self.specs, self.groups, self.weights = [], [], [], []
        for held, parts, offset in slots:
            for side in range(2):
                group = []
                for array, at in parts:
                    column = at + side * (array.shape[1] // (2 * wide))
                    group.append(len(self.arrays))
                    self.arrays.append(array)
                    self.specs.append(pl.BlockSpec((rows, wide), functools.partial(self.fixed, column)))
                self.groups.append(group)
        for held, parts, offset in slots:
            for side in range(2):
                if held not in weighted:
                    self.weights.append(None)
                    continue
                at = side * per_core + offset // wide
                self.weights.append(len(self.arrays))
                self.arrays.append(weight)
                self.specs.append(
                    pl.BlockSpec((tile, wide), functools.partial(self.placed, held, 2 * per_core, at))
                )

    @staticmethod
    def fixed(column, i, place):
        return (0, column)

    @staticmethod
    def placed(held, blocks, at, i, place):
        return (i, place[held] * blocks + at)

    def values(self, refs, place_ref):
        second = place_ref[7] == 1
        sides = [read_pick([refs[n] for n in group], second) for group in self.groups]
        return [jnp.concatenate(sides[n : n + 2], axis=1) for n in range(0, len(sides), 2)]

    def weight_values(self, refs):
        sides = [None if n is None else refs[n][...] for n in self.weights]
        return [
            None if sides[n] is None else jnp.concatenate(sides[n : n + 2], axis=1)
            for n in range(0, len(sides), 2)
        ]


def project_kernel(place_ref, *refs, operands, products, earlier, carried, joined):
    count = len(operands.arrays)
    blocks, rest = refs[:count], list(refs[count + earlier :])
    values = operands.values(blocks, place_ref)
    if "outer" in products:
        gated_ref = rest.pop(0)
        other_ref = rest.pop() if joined else None
        outs = [rest.pop() for _ in range(2 if joined else 4)][::-1]
        first_core, first_keeps = place_ref[4] == 0, place_ref[5] == 0
        wide = outs[0].shape[1]
        outers = [dot(gated_ref[...], value).astype(BF16) for value in values]
        outers = [
            jnp.where(first_keeps, outers[0], outers[1]),
            jnp.where(first_keeps, outers[1], outers[0]),
        ]
        for n, outer in enumerate(outers):
            left, right = outer[:, :wide], outer[:, wide:]
            other = jnp.where(first_core, right, left)
            if joined:
                outs[n][...] = jnp.where(first_core, left, right)
                other_ref[:, n * wide : (n + 1) * wide] = other
            else:
                outs[2 * n][...] = jnp.where(first_core, left, right)
                outs[2 * n + 1][...] = other
    if "inner" in products:
        total = rest.pop(0)[...] if carried else None
        for value, weight in zip(values, operands.weight_values(blocks)):
            if weight is not None:
                part = pair_dot(value, weight)
                total = part if total is None else total + part
        rest[0][...] = total


def project(place, slots, gated_t, weight, acc, wide, products, earlier, weighted, micros=100, joined=False):
    chans, rows = gated_t.shape
    tile = min(256 if "inner" in products else 512, chans)
    operands = Operands(slots, weight, tile, wide, weighted)
    col = pl.BlockSpec((rows, tile), lambda i, p: (0, i))
    carried = "inner" in products and acc is not None
    outs, out_specs, specs, arrays = [], [], [], []
    if "outer" in products:
        specs.append(pl.BlockSpec((tile, rows), lambda i, p: (i, 0)))
        arrays.append(gated_t)
    if "inner" in products:
        outs.append(jax.ShapeDtypeStruct((rows, chans), F32))
        out_specs.append(col)
        if carried:
            specs.append(col)
            arrays.append(acc)
    if "outer" in products:
        sizes = [wide, wide, 2 * wide] if joined else [wide] * 4
        outs += [jax.ShapeDtypeStruct((chans, size), BF16) for size in sizes]
        out_specs += [pl.BlockSpec((tile, size), lambda i, p: (i, 0)) for size in sizes]
    return pl.pallas_call(
        functools.partial(
            project_kernel, operands=operands, products=products, earlier=len(earlier), carried=carried,
            joined=joined,
        ),
        grid_spec=pltpu.PrefetchScalarGridSpec(
            num_scalar_prefetch=1,
            grid=(chans // tile,),
            in_specs=operands.specs + [ANYWHERE] * len(earlier) + specs,
            out_specs=out_specs,
        ),
        out_shape=outs,
        compiler_params=pltpu.CompilerParams(vmem_limit_bytes=VMEM_LIMIT),
        cost_estimate=weight_of(micros),
        name="project",
    )(place, *operands.arrays, *earlier, *arrays)


def grad_kernel(place_ref, *refs, operands, earlier, scale):
    count = len(operands.arrays) if operands else 0
    blocks = refs[:count]
    count += earlier
    acc_ref, conv_ref, q_ref, k_ref, v_ref, start_ref, before_ref, taps_ref, fwd_ref, inv_ref, lag_ref = refs[
        count : count + 11
    ]
    gq_ref, gk_ref, gv_ref, first_ref, last_ref, *gf_refs = refs[count + 11 :]
    span, chans = taps_ref.shape
    taps = to_freq(fwd_ref[...], taps_ref[...])
    tr, ti = taps[:span], taps[span:]
    acc_r = jnp.zeros((span, chans), F32)
    acc_i = jnp.zeros((span, chans), F32)
    if operands:
        value = jnp.concatenate(operands.values(blocks, place_ref), axis=1)
        weight = jnp.concatenate(operands.weight_values(blocks), axis=1)
        added = pair_dot(value, weight)
    last = q_ref.shape[0] // span - 1
    halo = jnp.where(start_ref[0] == 1, jnp.zeros_like(before_ref), before_ref[...])
    prev_mixed = to_freq(fwd_ref[...], halo)
    prev = None
    for b in range(last + 1):
        rows = pl.ds(b * span, span)
        gg = acc_ref[rows, :]
        if operands:
            gg = gg + added[b * span : (b + 1) * span]
        gq_ref[rows, :] = gg * conv_ref[rows, :].astype(F32)
        grad_conv = (gg * q_ref[rows, :].astype(F32)).astype(BF16)
        if b == 0:
            first_ref[...] = grad_conv
        if b == last:
            last_ref[...] = grad_conv
        grad = to_freq(fwd_ref[...], grad_conv)
        mixed = (k_ref[rows, :].astype(F32) * v_ref[rows, :].astype(F32)).astype(BF16)
        cur = to_freq(fwd_ref[...], mixed)
        xr, xi = window(prev_mixed, cur)
        prev_mixed = cur
        gr, gi = grad[:span], grad[span:]
        acc_r += gr * xr + gi * xi
        acc_i += gr * xi - gi * xr
        if b > 0:
            rows = pl.ds((b - 1) * span, span)
            back = filtered_back(prev, grad, tr, ti, inv_ref[...])
            gk_ref[rows, :] = back * v_ref[rows, :].astype(F32)
            gv_ref[rows, :] = back * k_ref[rows, :].astype(F32)
        prev = grad
    part = from_freq(lag_ref[...], jnp.concatenate([acc_r, acc_i], axis=0), 3) * scale
    if operands:
        even_ref, odd_ref = gf_refs
        wide = chans // 2
        first_core = place_ref[4] == 0
        away = pl.program_id(0) ^ place_ref[8]
        even_ref[away] = jnp.where(first_core, part[:, :wide], part[:, wide:])
        odd_ref[away] = jnp.where(first_core, part[:, wide:], part[:, :wide])
    else:
        gf_refs[0][...] = part


def filtered_back(cur, later, tr, ti, stack):
    wr, wi = window(cur, later)
    return from_freq(stack, jnp.concatenate([wr * tr + wi * ti, wi * tr - wr * ti], axis=0), 1)


def gradients(
    place, slots, weight, wide, acc, conv, query, key, value, is_start, before, taps, consts, scale, earlier
):
    rows, chans = query.shape
    span = taps.shape[0]
    tile = min(256, chans)
    fwd, stacks = consts
    operands = Operands(slots, weight, tile, wide, [held for held, _, _ in slots]) if slots else None
    col = pl.BlockSpec((rows, tile), lambda i, p: (0, i))
    short = pl.BlockSpec((span, tile), lambda i, p: (0, i))
    whole = pl.BlockSpec((2 * span, 2 * span), lambda i, p: (0, 0))
    return pl.pallas_call(
        functools.partial(grad_kernel, operands=operands, earlier=len(earlier), scale=scale),
        grid_spec=pltpu.PrefetchScalarGridSpec(
            num_scalar_prefetch=1,
            grid=(chans // tile,),
            in_specs=(operands.specs if slots else [])
            + [ANYWHERE] * len(earlier)
            + [col, col, col, col, col, SCALAR, short, short, whole, whole, whole],
            out_specs=[
                col,
                col,
                col,
                short,
                short,
            ]
            + ([pl.BlockSpec((4, span, tile // 2), lambda i, p: (0, 0, 0))] * 2 if slots else [short]),
        ),
        out_shape=[jax.ShapeDtypeStruct((rows, chans), F32)] * 3
        + [
            jax.ShapeDtypeStruct((span, chans), BF16),
            jax.ShapeDtypeStruct((span, chans), BF16),
        ]
        + (
            [jax.ShapeDtypeStruct((4, span, tile // 2), F32)] * 2
            if slots
            else [jax.ShapeDtypeStruct((span, chans), F32)]
        ),
        compiler_params=pltpu.CompilerParams(vmem_limit_bytes=VMEM_LIMIT),
        cost_estimate=weight_of(100),
        name="gradients",
    )(
        place, *(operands.arrays if slots else []), *earlier,
        acc, conv, query, key, value, is_start, before, taps, fwd, stacks[1], stacks[2],
    )


def last_kernel(end_ref, last_ref, after_ref, k_ref, v_ref, taps_ref, fwd_ref, inv_ref, gk_in, gv_in, gk_ref, gv_ref):
    span = taps_ref.shape[0]
    taps = to_freq(fwd_ref[...], taps_ref[...])
    cur = to_freq(fwd_ref[...], last_ref[...])
    later = to_freq(fwd_ref[...], jnp.where(end_ref[0] == 1, jnp.zeros_like(after_ref), after_ref[...]))
    back = filtered_back(cur, later, taps[:span], taps[span:], inv_ref[...])
    gk_ref[...] = back * v_ref[...].astype(F32)
    gv_ref[...] = back * k_ref[...].astype(F32)


def last_rows(is_end, last, after_rows, key, value, taps, grad_key, grad_value, consts):
    rows, chans = key.shape
    span = taps.shape[0]
    tile = min(512, chans)
    fwd, stacks = consts
    bottom = rows // span - 1
    low = pl.BlockSpec((span, tile), lambda i: (bottom, i))
    short = pl.BlockSpec((span, tile), lambda i: (0, i))
    whole = pl.BlockSpec((2 * span, 2 * span), lambda i: (0, 0))
    return pl.pallas_call(
        last_kernel,
        grid=(chans // tile,),
        in_specs=[
            SCALAR, short, short, low, low, short, whole, whole, ANYWHERE, ANYWHERE,
        ],
        out_specs=[low, low],
        out_shape=[jax.ShapeDtypeStruct((rows, chans), F32)] * 2,
        input_output_aliases={8: 0, 9: 1},
        compiler_params=pltpu.CompilerParams(vmem_limit_bytes=VMEM_LIMIT),
        cost_estimate=weight_of(2),
        name="last_rows",
    )(is_end, last, after_rows, key, value, taps, fwd, stacks[1], grad_key, grad_value)


def finish_kernel(early_ref, *refs, own, groups, across, scale):
    out = refs[-1]
    for cols, late in group_sums(refs[own:], groups, across):
        early = sum(ref[:, cols].astype(F32) for ref in refs[:own])
        out[:, cols] = jnp.where(early_ref[0] == 1, early, late) * scale


def finish(is_early, own_terms, groups, across, out, at, scale):
    rows, wide = across[0].shape
    tile = rows // 2
    terms = [term for group in groups for term in group] + list(across)
    sizes = [(len(group), group[0].shape[1]) for group in groups]
    block = pl.BlockSpec((tile, wide), lambda i, p: (i, at))
    held = [] if out is None else [out]
    return pl.pallas_call(
        functools.partial(finish_kernel, own=len(own_terms), groups=sizes, across=len(across), scale=scale),
        grid_spec=pltpu.PrefetchScalarGridSpec(
            num_scalar_prefetch=1,
            grid=(rows // tile,),
            in_specs=[block] * len(own_terms)
            + [half_spec(term, tile) for term in terms]
            + [ANYWHERE] * len(held),
            out_specs=block,
        ),
        out_shape=jax.ShapeDtypeStruct((rows, own_terms[0].shape[1]), F32),
        input_output_aliases={1 + len(own_terms) + len(terms): 0} if held else {},
        compiler_params=pltpu.CompilerParams(vmem_limit_bytes=VMEM_LIMIT),
        cost_estimate=weight_of(2),
        name="finish",
    )(is_early, *own_terms, *bare(terms), *held)


def on_line(pairs, contexts):
    return [(a * contexts + c, b * contexts + c) for a, b in pairs for c in range(contexts)]


def send_line(value, pairs, contexts):
    return lax.ppermute(value, ("tensor", "context"), on_line(pairs, contexts))


def swap(value, bit, contexts):
    return lax.ppermute(value, "context", [(c, c ^ bit) for c in range(contexts)])


def pieces_kernel(*refs, pieces):
    outs = refs[-len(pieces) :]
    half = refs[0].shape[1] // 2
    for (offset, wide), out in zip(pieces, outs):
        for side in range(2):
            at = side * half + offset
            out[:, side * wide : (side + 1) * wide] = refs[0][:, at : at + wide]


def cut(block, pieces, earlier):
    rows, chans = block.shape
    return pl.pallas_call(
        functools.partial(pieces_kernel, pieces=pieces),
        grid=(4,),
        in_specs=[pl.BlockSpec((rows // 4, chans), lambda i: (i, 0))] + [ANYWHERE] * len(earlier),
        out_specs=[pl.BlockSpec((rows // 4, 2 * wide), lambda i: (i, 0)) for _, wide in pieces],
        out_shape=[jax.ShapeDtypeStruct((rows, 2 * wide), BF16) for _, wide in pieces],
        cost_estimate=weight_of(100),
        name="cut",
    )(block, *earlier)


def hold_kernel(*refs):
    pass


def hold(value, earlier):
    return pl.pallas_call(
        hold_kernel,
        in_specs=[ANYWHERE] * (1 + len(earlier)),
        out_specs=ANYWHERE,
        out_shape=jax.ShapeDtypeStruct(value.shape, value.dtype),
        input_output_aliases={0: 0},
        cost_estimate=weight_of(1),
        name="hold",
    )(value, *earlier)


def group_sums(refs, groups, across):
    at, column, wide_refs = 0, 0, refs[sum(count for count, _ in groups) :][:across]
    for count, wide in groups:
        cols = slice(column, column + wide)
        terms = [ref[...] for ref in refs[at : at + count]] + [ref[:, cols] for ref in wide_refs]
        yield cols, sum(term.astype(F32) for term in terms)
        at, column = at + count, column + wide


def half_spec(term, tile):
    array, at = term if isinstance(term, tuple) else (term, None)
    wide = array.shape[1] if at is None else array.shape[1] // 2
    return pl.BlockSpec((tile, wide), lambda i, *_: (i, at or 0))


def bare(terms):
    return [term[0] if isinstance(term, tuple) else term for term in terms]


def add_kernel(*refs, groups, across):
    for cols, total in group_sums(refs, groups, across):
        refs[-1][:, cols] = total.astype(BF16)


def add_blocks(groups, earlier, micros=1, across=()):
    rows = groups[0][0].shape[0]
    tile = rows // 2
    terms = [term for group in groups for term in group] + list(across)
    sizes = [(len(group), group[0].shape[1]) for group in groups]
    wide = sum(size for _, size in sizes)
    return pl.pallas_call(
        functools.partial(add_kernel, groups=sizes, across=len(across)),
        grid=(rows // tile,),
        in_specs=[half_spec(term, tile) for term in terms] + [ANYWHERE] * len(earlier),
        out_specs=pl.BlockSpec((tile, wide), lambda i: (i, 0)),
        out_shape=jax.ShapeDtypeStruct((rows, wide), BF16),
        compiler_params=pltpu.CompilerParams(vmem_limit_bytes=VMEM_LIMIT),
        cost_estimate=weight_of(micros),
        name="add_blocks",
    )(*bare(terms), *earlier)


def body(query, key, value, taps, weight, out_grad, tensors, contexts):
    rows, chans = query.shape
    span = taps.shape[0]
    scale = 1.0 / math.sqrt(rows * contexts)
    consts = odd_dft(span)
    ctx = lax.axis_index("context")
    ten = lax.axis_index("tensor")

    tail = lambda x: x[rows - span :].astype(F32)
    last_mixed = (tail(key) * tail(value)).astype(BF16)
    before = lax.ppermute(last_mixed, "context", [(c, (c + 1) % contexts) for c in range(contexts)])
    is_start = (ctx == 0).astype(jnp.int32).reshape(1)
    is_end = (ctx == contexts - 1).astype(jnp.int32).reshape(1)

    def complete(first, last, grad_key, grad_value):
        after_rows = lax.ppermute(first, "context", [(c, (c - 1) % contexts) for c in range(contexts)])
        return last_rows(is_end, last, after_rows, key, value, taps, grad_key, grad_value, consts)

    if tensors == 4 and contexts == 8 and chans == 1024:
        half = chans // 2
        pieces = [(0, half // 2), (half // 2, half // 4), (3 * half // 4, half // 4)]
        chip, core = ctx // 2, lax.rem(ctx, 2)
        low = ten < 2
        edge = (ten == 0) | (ten == 3)
        held = [ten, ten ^ 1, jnp.where(low, 2, 1), jnp.where(low, 3, 0)]
        sides = [(h ^ chip) & 1 for h in held]
        early = jnp.stack(held + [core] + sides[:2] + [edge]).astype(jnp.int32)
        late = jnp.stack(held + [core] + sides[2:] + [edge, chip]).astype(jnp.int32)
        is_early = ((chip // 2) == (ten // 2)).astype(jnp.int32).reshape(1)

        swap_ends = [(0, 1), (1, 0), (2, 3), (3, 2)]
        swap_mid = [(1, 2), (2, 1)]
        over = lambda value, bit: swap(value, bit, contexts)
        pair = send_line(out_grad, swap_ends, contexts)
        near_mid = send_line(out_grad, swap_mid, contexts)
        conv, gated_t = filtered(is_start, query, key, value, before, taps, consts)
        near_end = send_line(near_mid, swap_ends, contexts)

        slots = [(0, [(out_grad, 0)], 0), (1, [(pair, 0)], 0)]
        gg, keep, other_keep, cross, other_cross = project(
            early, slots, gated_t, weight, None, half, ("outer", "inner"), [near_mid], [0, 1]
        )
        far_mid = [send_line(block, swap_mid, contexts) for block in cut(pair, pieces, [gg])]
        far_end = [send_line(block, swap_ends, contexts) for block in far_mid]
        cross_in = add_blocks([[cross, over(other_cross, 1)]], [])
        own_terms = [keep, over(other_keep, 1), over(cross_in, 2)]

        slots = [(2, [(near_mid, 0), (near_end, 0)], 0)]
        (gg,) = project(late, slots, gated_t, weight, gg, half, ("inner",), [cross_in], [2])
        own_in = add_blocks([own_terms], [gg])
        own_terms.append(over(own_in, 4))

        keeps, crosses = [], []
        for n, (offset, wide) in enumerate(pieces):
            slots = [
                (2, [(near_mid, offset // wide), (near_end, offset // wide)], offset),
                (3, [(far_mid[n], 0), (far_end[n], 0)], offset),
            ]
            if n == 0:
                gg, *outer = project(
                    late, slots, gated_t, weight, gg, wide, ("outer", "inner"), [own_in], [3]
                )
            else:
                earlier = [] if n == 1 else [gg, own_terms[-1]]
                outer = project(late, slots, gated_t, weight, None, wide, ("outer",), earlier, [], joined=True)
            if n == 0:
                keep, other_keep, cross, other_cross = outer
                keeps.append([keep, over(other_keep, 1)])
                crosses.append([cross, over(other_cross, 1)])
            else:
                keep, cross, other = outer
                got = over(other, 1)
                keeps.append([keep, (got, 0)])
                crosses.append([cross, (got, 1)])
            if n == 1:
                first_cross = add_blocks([crosses[0]], [keep], 0.1)
                keeps[0].append(over(first_cross, 2))
                (gg,) = project(
                    late, slots[1:], gated_t, weight, gg, wide, ("inner",), [first_cross], [3], 0.1
                )
        first_in = add_blocks([keeps[0]], [])
        last_cross = add_blocks(crosses[1:], [first_in])
        last_over = over(last_cross, 2)
        grad_query, grad_key, grad_value, first, last, even, odd = gradients(
            late, slots[1:], weight, wide, gg, conv, query, key, value, is_start, before, taps, consts,
            scale, [last_cross],
        )
        first_over = over(first_in, 4)
        grad_weight = finish(is_early, own_terms, keeps[:1], [first_over], None, 0, scale)
        last_in = add_blocks(keeps[1:], [first, first_over], 1, [last_over])
        last_over_y = over(last_in, 4)
        got = over(hold(odd, [last_in]), 1)
        grad_key, grad_value = complete(first, last, grad_key, grad_value)
        got = hold(got, [last_over_y, grad_weight, grad_key])
        grad_filter = even[0] + got[0] + sum(over(even[n] + got[n], 2 * n) for n in (1, 2, 3))
        grad_weight = finish(
            is_early, own_terms, keeps[1:], [last_over, last_over_y], grad_weight, 1, scale
        )
    else:
        conv, gated_t = filtered(is_start, query, key, value, before, taps, consts)
        segment = lax.all_gather(out_grad, "tensor", axis=1, tiled=True)
        gg = lax.dot_general(segment, weight, (((1,), (1,)), ((), ())), preferred_element_type=F32)
        outer = dot(gated_t, segment)
        grad_weight = lax.psum_scatter(outer, "context", scatter_dimension=1, tiled=True) * scale
        grad_query, grad_key, grad_value, first, last, part = gradients(
            jnp.zeros((1,), jnp.int32), None, weight, 0, gg, conv, query, key, value, is_start, before, taps, consts,
            scale, [],
        )
        grad_filter = lax.psum_scatter(part, "context", scatter_dimension=1, tiled=True)
        grad_key, grad_value = complete(first, last, grad_key, grad_value)


    return (grad_query, grad_key, grad_value, grad_filter, grad_weight)


def solution(mesh):
    placed = (
        P("context", "tensor"),
        P("context", "tensor"),
        P("context", "tensor"),
        P(None, "tensor"),
        P("tensor", None),
        P("context", "tensor"),
    )
    run = functools.partial(body, tensors=mesh.shape["tensor"], contexts=mesh.shape["context"])
    return jax.shard_map(
        run,
        mesh=mesh,
        in_specs=placed,
        out_specs=(
            P("context", "tensor"),
            P("context", "tensor"),
            P("context", "tensor"),
            P(None, ("tensor", "context")),
            P("tensor", "context"),
        ),
        check_vma=False,
    )
```

```python
import functools
import math

import jax
import jax.numpy as jnp
import numpy as np
from jax import lax
from jax.experimental import pallas as pl
from jax.experimental.pallas import tpu as pltpu
from jax.sharding import PartitionSpec as P

BF16 = jnp.bfloat16
F32 = jnp.float32
VMEM_LIMIT = 48 * 1024 * 1024

ANYWHERE = pl.BlockSpec(memory_space=pl.ANY)
SCALAR = pl.BlockSpec(memory_space=pltpu.SMEM)


def weight_of(micros):
    return pl.CostEstimate(flops=1 << 20, bytes_accessed=int(micros * 3.7e6), transcendentals=0)


def split_const(matrix):
    high = matrix.astype(np.float32).astype(jnp.bfloat16)
    low = (matrix - high.astype(np.float64)).astype(np.float32).astype(jnp.bfloat16)
    return high, low


def odd_dft(span):
    freq = np.pi * (np.arange(span) + 0.5) / span * (1 - 2 * (np.arange(span) % 2))
    pos = np.arange(span)
    ahead = np.outer(freq, pos)
    forward = np.concatenate([np.cos(ahead), -np.sin(ahead)], axis=0)

    def backward(at):
        angle = np.outer(at, freq)
        return np.concatenate([np.cos(angle), -np.sin(angle)], axis=1) / span

    f_high, f_low = split_const(forward)
    stacks = []
    for at in (span + pos, pos, span - pos):
        b_high, b_low = split_const(backward(at))
        stacks.append(np.concatenate([b_high, b_low], axis=0))
    return np.concatenate([f_high, f_low], axis=1), stacks


def dot(lhs, rhs):
    return jnp.dot(lhs, rhs, preferred_element_type=F32)


def to_freq(fwd, block):
    return dot(fwd, jnp.concatenate([block, block], axis=0))


def from_freq(stack, value, passes):
    span = stack.shape[0] // 2
    high = value.astype(BF16)
    if passes == 1:
        return dot(stack[:span], high)
    both = dot(stack, high)
    total = both[:span] + both[span:]
    if passes == 3:
        total = total + dot(stack[:span], (value - high.astype(F32)).astype(BF16))
    return total


def window(first, second):
    span = first.shape[0] // 2
    real = first[:span] + second[span:]
    imag = first[span:] - second[:span]
    return real, imag


def conv_kernel(start_ref, q_ref, k_ref, v_ref, halo_ref, taps_ref, fwd_ref, inv_ref, conv_ref, gated_ref):
    span = taps_ref.shape[0]
    taps = to_freq(fwd_ref[...], taps_ref[...])
    tr, ti = taps[:span], taps[span:]
    halo = jnp.where(start_ref[0] == 1, jnp.zeros_like(halo_ref), halo_ref[...])
    prev = to_freq(fwd_ref[...], halo)
    for b in range(q_ref.shape[0] // span):
        rows = pl.ds(b * span, span)
        mixed = (k_ref[rows, :].astype(F32) * v_ref[rows, :].astype(F32)).astype(BF16)
        cur = to_freq(fwd_ref[...], mixed)
        xr, xi = window(prev, cur)
        spec = jnp.concatenate([xr * tr - xi * ti, xr * ti + xi * tr], axis=0)
        conv = from_freq(inv_ref[...], spec, 3)
        conv_ref[rows, :] = conv.astype(BF16)
        gated_ref[:, rows] = jnp.transpose(q_ref[rows, :].astype(F32) * conv).astype(BF16)
        prev = cur


def filtered(is_start, query, key, value, halo, taps, consts):
    rows, chans = query.shape
    span = taps.shape[0]
    tile = min(256, chans)
    fwd, stacks = consts
    col = pl.BlockSpec((rows, tile), lambda i: (0, i))
    short = pl.BlockSpec((span, tile), lambda i: (0, i))
    whole = pl.BlockSpec((2 * span, 2 * span), lambda i: (0, 0))
    return pl.pallas_call(
        conv_kernel,
        grid=(chans // tile,),
        in_specs=[SCALAR, col, col, col, short, short, whole, whole],
        out_specs=[
            col,
            pl.BlockSpec((tile, rows), lambda i: (i, 0)),
        ],
        out_shape=[
            jax.ShapeDtypeStruct((rows, chans), BF16),
            jax.ShapeDtypeStruct((chans, rows), BF16),
        ],
        compiler_params=pltpu.CompilerParams(vmem_limit_bytes=VMEM_LIMIT),
        cost_estimate=weight_of(100),
        name="filtered",
    )(is_start, query, key, value, halo, taps, fwd, stacks[0])


def pair_dot(lhs, rhs):
    return lax.dot_general(lhs, rhs, (((1,), (1,)), ((), ())), preferred_element_type=F32)


def read_pick(refs, second):
    value = refs[0][...]
    for ref in refs[1:]:
        value = jnp.where(second, ref[...], value)
    return value


class Operands:
    def __init__(self, slots, weight, tile, wide, weighted):
        rows = slots[0][1][0][0].shape[0]
        per_core = weight.shape[0] // (2 * wide)
        self.arrays, self.specs, self.groups, self.weights = [], [], [], []
        for held, parts, offset in slots:
            for side in range(2):
                group = []
                for array, at in parts:
                    column = at + side * (array.shape[1] // (2 * wide))
                    group.append(len(self.arrays))
                    self.arrays.append(array)
                    self.specs.append(pl.BlockSpec((rows, wide), functools.partial(self.fixed, column)))
                self.groups.append(group)
        for held, parts, offset in slots:
            for side in range(2):
                if held not in weighted:
                    self.weights.append(None)
                    continue
                at = side * per_core + offset // wide
                self.weights.append(len(self.arrays))
                self.arrays.append(weight)
                self.specs.append(
                    pl.BlockSpec((tile, wide), functools.partial(self.placed, held, 2 * per_core, at))
                )

    @staticmethod
    def fixed(column, i, place):
        return (0, column)

    @staticmethod
    def placed(held, blocks, at, i, place):
        return (i, place[held] * blocks + at)

    def values(self, refs, place_ref):
        second = place_ref[7] == 1
        sides = [read_pick([refs[n] for n in group], second) for group in self.groups]
        return [jnp.concatenate(sides[n : n + 2], axis=1) for n in range(0, len(sides), 2)]

    def weight_values(self, refs):
        sides = [None if n is None else refs[n][...] for n in self.weights]
        return [
            None if sides[n] is None else jnp.concatenate(sides[n : n + 2], axis=1)
            for n in range(0, len(sides), 2)
        ]


def project_kernel(place_ref, *refs, operands, products, earlier, carried, joined):
    count = len(operands.arrays)
    blocks, rest = refs[:count], list(refs[count + earlier :])
    values = operands.values(blocks, place_ref)
    if "outer" in products:
        gated_ref = rest.pop(0)
        other_ref = rest.pop() if joined else None
        outs = [rest.pop() for _ in range(2 if joined else 4)][::-1]
        first_core, first_keeps = place_ref[4] == 0, place_ref[5] == 0
        wide = outs[0].shape[1]
        outers = [dot(gated_ref[...], value).astype(BF16) for value in values]
        outers = [
            jnp.where(first_keeps, outers[0], outers[1]),
            jnp.where(first_keeps, outers[1], outers[0]),
        ]
        for n, outer in enumerate(outers):
            left, right = outer[:, :wide], outer[:, wide:]
            other = jnp.where(first_core, right, left)
            if joined:
                outs[n][...] = jnp.where(first_core, left, right)
                other_ref[:, n * wide : (n + 1) * wide] = other
            else:
                outs[2 * n][...] = jnp.where(first_core, left, right)
                outs[2 * n + 1][...] = other
    if "inner" in products:
        total = rest.pop(0)[...] if carried else None
        for value, weight in zip(values, operands.weight_values(blocks)):
            if weight is not None:
                part = pair_dot(value, weight)
                total = part if total is None else total + part
        rest[0][...] = total


def project(place, slots, gated_t, weight, acc, wide, products, earlier, weighted, micros=100, joined=False):
    chans, rows = gated_t.shape
    tile = min(256 if "inner" in products else 512, chans)
    operands = Operands(slots, weight, tile, wide, weighted)
    col = pl.BlockSpec((rows, tile), lambda i, p: (0, i))
    carried = "inner" in products and acc is not None
    outs, out_specs, specs, arrays = [], [], [], []
    if "outer" in products:
        specs.append(pl.BlockSpec((tile, rows), lambda i, p: (i, 0)))
        arrays.append(gated_t)
    if "inner" in products:
        outs.append(jax.ShapeDtypeStruct((rows, chans), F32))
        out_specs.append(col)
        if carried:
            specs.append(col)
            arrays.append(acc)
    if "outer" in products:
        sizes = [wide, wide, 2 * wide] if joined else [wide] * 4
        outs += [jax.ShapeDtypeStruct((chans, size), BF16) for size in sizes]
        out_specs += [pl.BlockSpec((tile, size), lambda i, p: (i, 0)) for size in sizes]
    return pl.pallas_call(
        functools.partial(
            project_kernel, operands=operands, products=products, earlier=len(earlier), carried=carried,
            joined=joined,
        ),
        grid_spec=pltpu.PrefetchScalarGridSpec(
            num_scalar_prefetch=1,
            grid=(chans // tile,),
            in_specs=operands.specs + [ANYWHERE] * len(earlier) + specs,
            out_specs=out_specs,
        ),
        out_shape=outs,
        compiler_params=pltpu.CompilerParams(vmem_limit_bytes=VMEM_LIMIT),
        cost_estimate=weight_of(micros),
        name="project",
    )(place, *operands.arrays, *earlier, *arrays)


def grad_kernel(place_ref, *refs, operands, earlier, scale):
    count = len(operands.arrays) if operands else 0
    blocks = refs[:count]
    count += earlier
    acc_ref, conv_ref, q_ref, k_ref, v_ref, start_ref, before_ref, taps_ref, fwd_ref, inv_ref, lag_ref = refs[
        count : count + 11
    ]
    gq_ref, gk_ref, gv_ref, first_ref, last_ref, *gf_refs = refs[count + 11 :]
    span, chans = taps_ref.shape
    taps = to_freq(fwd_ref[...], taps_ref[...])
    tr, ti = taps[:span], taps[span:]
    acc_r = jnp.zeros((span, chans), F32)
    acc_i = jnp.zeros((span, chans), F32)
    if operands:
        value = jnp.concatenate(operands.values(blocks, place_ref), axis=1)
        weight = jnp.concatenate(operands.weight_values(blocks), axis=1)
        added = pair_dot(value, weight)
    last = q_ref.shape[0] // span - 1
    halo = jnp.where(start_ref[0] == 1, jnp.zeros_like(before_ref), before_ref[...])
    prev_mixed = to_freq(fwd_ref[...], halo)
    prev = None
    for b in range(last + 1):
        rows = pl.ds(b * span, span)
        gg = acc_ref[rows, :]
        if operands:
            gg = gg + added[b * span : (b + 1) * span]
        gq_ref[rows, :] = gg * conv_ref[rows, :].astype(F32)
        grad_conv = (gg * q_ref[rows, :].astype(F32)).astype(BF16)
        if b == 0:
            first_ref[...] = grad_conv
        if b == last:
            last_ref[...] = grad_conv
        grad = to_freq(fwd_ref[...], grad_conv)
        mixed = (k_ref[rows, :].astype(F32) * v_ref[rows, :].astype(F32)).astype(BF16)
        cur = to_freq(fwd_ref[...], mixed)
        xr, xi = window(prev_mixed, cur)
        prev_mixed = cur
        gr, gi = grad[:span], grad[span:]
        acc_r += gr * xr + gi * xi
        acc_i += gr * xi - gi * xr
        if b > 0:
            rows = pl.ds((b - 1) * span, span)
            back = filtered_back(prev, grad, tr, ti, inv_ref[...])
            gk_ref[rows, :] = back * v_ref[rows, :].astype(F32)
            gv_ref[rows, :] = back * k_ref[rows, :].astype(F32)
        prev = grad
    part = from_freq(lag_ref[...], jnp.concatenate([acc_r, acc_i], axis=0), 3) * scale
    if operands:
        even_ref, odd_ref = gf_refs
        wide = chans // 2
        first_core = place_ref[4] == 0
        away = pl.program_id(0) ^ place_ref[8]
        even_ref[away] = jnp.where(first_core, part[:, :wide], part[:, wide:])
        odd_ref[away] = jnp.where(first_core, part[:, wide:], part[:, :wide])
    else:
        gf_refs[0][...] = part


def filtered_back(cur, later, tr, ti, stack):
    wr, wi = window(cur, later)
    return from_freq(stack, jnp.concatenate([wr * tr + wi * ti, wi * tr - wr * ti], axis=0), 1)


def gradients(
    place, slots, weight, wide, acc, conv, query, key, value, is_start, before, taps, consts, scale, earlier
):
    rows, chans = query.shape
    span = taps.shape[0]
    tile = min(256, chans)
    fwd, stacks = consts
    operands = Operands(slots, weight, tile, wide, [held for held, _, _ in slots]) if slots else None
    col = pl.BlockSpec((rows, tile), lambda i, p: (0, i))
    short = pl.BlockSpec((span, tile), lambda i, p: (0, i))
    whole = pl.BlockSpec((2 * span, 2 * span), lambda i, p: (0, 0))
    return pl.pallas_call(
        functools.partial(grad_kernel, operands=operands, earlier=len(earlier), scale=scale),
        grid_spec=pltpu.PrefetchScalarGridSpec(
            num_scalar_prefetch=1,
            grid=(chans // tile,),
            in_specs=(operands.specs if slots else [])
            + [ANYWHERE] * len(earlier)
            + [col, col, col, col, col, SCALAR, short, short, whole, whole, whole],
            out_specs=[
                col,
                col,
                col,
                short,
                short,
            ]
            + ([pl.BlockSpec((4, span, tile // 2), lambda i, p: (0, 0, 0))] * 2 if slots else [short]),
        ),
        out_shape=[jax.ShapeDtypeStruct((rows, chans), F32)] * 3
        + [
            jax.ShapeDtypeStruct((span, chans), BF16),
            jax.ShapeDtypeStruct((span, chans), BF16),
        ]
        + (
            [jax.ShapeDtypeStruct((4, span, tile // 2), F32)] * 2
            if slots
            else [jax.ShapeDtypeStruct((span, chans), F32)]
        ),
        compiler_params=pltpu.CompilerParams(vmem_limit_bytes=VMEM_LIMIT),
        cost_estimate=weight_of(100),
        name="gradients",
    )(
        place, *(operands.arrays if slots else []), *earlier,
        acc, conv, query, key, value, is_start, before, taps, fwd, stacks[1], stacks[2],
    )


def last_kernel(end_ref, last_ref, after_ref, k_ref, v_ref, taps_ref, fwd_ref, inv_ref, gk_in, gv_in, gk_ref, gv_ref):
    span = taps_ref.shape[0]
    taps = to_freq(fwd_ref[...], taps_ref[...])
    cur = to_freq(fwd_ref[...], last_ref[...])
    later = to_freq(fwd_ref[...], jnp.where(end_ref[0] == 1, jnp.zeros_like(after_ref), after_ref[...]))
    back = filtered_back(cur, later, taps[:span], taps[span:], inv_ref[...])
    gk_ref[...] = back * v_ref[...].astype(F32)
    gv_ref[...] = back * k_ref[...].astype(F32)


def last_rows(is_end, last, after_rows, key, value, taps, grad_key, grad_value, consts):
    rows, chans = key.shape
    span = taps.shape[0]
    tile = min(512, chans)
    fwd, stacks = consts
    bottom = rows // span - 1
    low = pl.BlockSpec((span, tile), lambda i: (bottom, i))
    short = pl.BlockSpec((span, tile), lambda i: (0, i))
    whole = pl.BlockSpec((2 * span, 2 * span), lambda i: (0, 0))
    return pl.pallas_call(
        last_kernel,
        grid=(chans // tile,),
        in_specs=[
            SCALAR, short, short, low, low, short, whole, whole, ANYWHERE, ANYWHERE,
        ],
        out_specs=[low, low],
        out_shape=[jax.ShapeDtypeStruct((rows, chans), F32)] * 2,
        input_output_aliases={8: 0, 9: 1},
        compiler_params=pltpu.CompilerParams(vmem_limit_bytes=VMEM_LIMIT),
        cost_estimate=weight_of(2),
        name="last_rows",
    )(is_end, last, after_rows, key, value, taps, fwd, stacks[1], grad_key, grad_value)


def finish_kernel(early_ref, *refs, own, groups, across, scale):
    out = refs[-1]
    for cols, late in group_sums(refs[own:], groups, across):
        early = sum(ref[:, cols].astype(F32) for ref in refs[:own])
        out[:, cols] = jnp.where(early_ref[0] == 1, early, late) * scale


def finish(is_early, own_terms, groups, across, out, at, scale):
    rows, wide = across[0].shape
    tile = rows // 2
    terms = [term for group in groups for term in group] + list(across)
    sizes = [(len(group), group[0].shape[1]) for group in groups]
    block = pl.BlockSpec((tile, wide), lambda i, p: (i, at))
    held = [] if out is None else [out]
    return pl.pallas_call(
        functools.partial(finish_kernel, own=len(own_terms), groups=sizes, across=len(across), scale=scale),
        grid_spec=pltpu.PrefetchScalarGridSpec(
            num_scalar_prefetch=1,
            grid=(rows // tile,),
            in_specs=[block] * len(own_terms)
            + [half_spec(term, tile) for term in terms]
            + [ANYWHERE] * len(held),
            out_specs=block,
        ),
        out_shape=jax.ShapeDtypeStruct((rows, own_terms[0].shape[1]), F32),
        input_output_aliases={1 + len(own_terms) + len(terms): 0} if held else {},
        compiler_params=pltpu.CompilerParams(vmem_limit_bytes=VMEM_LIMIT),
        cost_estimate=weight_of(2),
        name="finish",
    )(is_early, *own_terms, *bare(terms), *held)


def on_line(pairs, contexts):
    return [(a * contexts + c, b * contexts + c) for a, b in pairs for c in range(contexts)]


def send_line(value, pairs, contexts):
    return lax.ppermute(value, ("tensor", "context"), on_line(pairs, contexts))


def swap(value, bit, contexts):
    return lax.ppermute(value, "context", [(c, c ^ bit) for c in range(contexts)])


def pieces_kernel(*refs, pieces):
    outs = refs[-len(pieces) :]
    half = refs[0].shape[1] // 2
    for (offset, wide), out in zip(pieces, outs):
        for side in range(2):
            at = side * half + offset
            out[:, side * wide : (side + 1) * wide] = refs[0][:, at : at + wide]


def cut(block, pieces, earlier):
    rows, chans = block.shape
    return pl.pallas_call(
        functools.partial(pieces_kernel, pieces=pieces),
        grid=(4,),
        in_specs=[pl.BlockSpec((rows // 4, chans), lambda i: (i, 0))] + [ANYWHERE] * len(earlier),
        out_specs=[pl.BlockSpec((rows // 4, 2 * wide), lambda i: (i, 0)) for _, wide in pieces],
        out_shape=[jax.ShapeDtypeStruct((rows, 2 * wide), BF16) for _, wide in pieces],
        cost_estimate=weight_of(100),
        name="cut",
    )(block, *earlier)


def hold_kernel(*refs):
    pass


def hold(value, earlier):
    return pl.pallas_call(
        hold_kernel,
        in_specs=[ANYWHERE] * (1 + len(earlier)),
        out_specs=ANYWHERE,
        out_shape=jax.ShapeDtypeStruct(value.shape, value.dtype),
        input_output_aliases={0: 0},
        cost_estimate=weight_of(1),
        name="hold",
    )(value, *earlier)


def group_sums(refs, groups, across):
    at, column, wide_refs = 0, 0, refs[sum(count for count, _ in groups) :][:across]
    for count, wide in groups:
        cols = slice(column, column + wide)
        terms = [ref[...] for ref in refs[at : at + count]] + [ref[:, cols] for ref in wide_refs]
        yield cols, sum(term.astype(F32) for term in terms)
        at, column = at + count, column + wide


def half_spec(term, tile):
    array, at = term if isinstance(term, tuple) else (term, None)
    wide = array.shape[1] if at is None else array.shape[1] // 2
    return pl.BlockSpec((tile, wide), lambda i, *_: (i, at or 0))


def bare(terms):
    return [term[0] if isinstance(term, tuple) else term for term in terms]


def add_kernel(*refs, groups, across):
    for cols, total in group_sums(refs, groups, across):
        refs[-1][:, cols] = total.astype(BF16)


def add_blocks(groups, earlier, micros=1, across=()):
    rows = groups[0][0].shape[0]
    tile = rows // 2
    terms = [term for group in groups for term in group] + list(across)
    sizes = [(len(group), group[0].shape[1]) for group in groups]
    wide = sum(size for _, size in sizes)
    return pl.pallas_call(
        functools.partial(add_kernel, groups=sizes, across=len(across)),
        grid=(rows // tile,),
        in_specs=[half_spec(term, tile) for term in terms] + [ANYWHERE] * len(earlier),
        out_specs=pl.BlockSpec((tile, wide), lambda i: (i, 0)),
        out_shape=jax.ShapeDtypeStruct((rows, wide), BF16),
        compiler_params=pltpu.CompilerParams(vmem_limit_bytes=VMEM_LIMIT),
        cost_estimate=weight_of(micros),
        name="add_blocks",
    )(*bare(terms), *earlier)


def body(query, key, value, taps, weight, out_grad, tensors, contexts):
    rows, chans = query.shape
    span = taps.shape[0]
    scale = 1.0 / math.sqrt(rows * contexts)
    consts = odd_dft(span)
    ctx = lax.axis_index("context")
    ten = lax.axis_index("tensor")

    tail = lambda x: x[rows - span :].astype(F32)
    last_mixed = (tail(key) * tail(value)).astype(BF16)
    before = lax.ppermute(last_mixed, "context", [(c, (c + 1) % contexts) for c in range(contexts)])
    is_start = (ctx == 0).astype(jnp.int32).reshape(1)
    is_end = (ctx == contexts - 1).astype(jnp.int32).reshape(1)

    def complete(first, last, grad_key, grad_value):
        after_rows = lax.ppermute(first, "context", [(c, (c - 1) % contexts) for c in range(contexts)])
        return last_rows(is_end, last, after_rows, key, value, taps, grad_key, grad_value, consts)

    if tensors == 4 and contexts == 8 and chans == 1024:
        half = chans // 2
        pieces = [(0, half // 2), (half // 2, half // 4), (3 * half // 4, half // 4)]
        chip, core = ctx // 2, lax.rem(ctx, 2)
        low = ten < 2
        edge = (ten == 0) | (ten == 3)
        held = [ten, ten ^ 1, jnp.where(low, 2, 1), jnp.where(low, 3, 0)]
        sides = [(h ^ chip) & 1 for h in held]
        early = jnp.stack(held + [core] + sides[:2] + [edge]).astype(jnp.int32)
        late = jnp.stack(held + [core] + sides[2:] + [edge, chip]).astype(jnp.int32)
        is_early = ((chip // 2) == (ten // 2)).astype(jnp.int32).reshape(1)

        swap_ends = [(0, 1), (1, 0), (2, 3), (3, 2)]
        swap_mid = [(1, 2), (2, 1)]
        over = lambda value, bit: swap(value, bit, contexts)
        pair = send_line(out_grad, swap_ends, contexts)
        near_mid = send_line(out_grad, swap_mid, contexts)
        conv, gated_t = filtered(is_start, query, key, value, before, taps, consts)
        near_end = send_line(near_mid, swap_ends, contexts)

        slots = [(0, [(out_grad, 0)], 0), (1, [(pair, 0)], 0)]
        gg, keep, other_keep, cross, other_cross = project(
            early, slots, gated_t, weight, None, half, ("outer", "inner"), [near_mid], [0, 1]
        )
        far_mid = [send_line(block, swap_mid, contexts) for block in cut(pair, pieces, [gg])]
        far_end = [send_line(block, swap_ends, contexts) for block in far_mid]
        cross_in = add_blocks([[cross, over(other_cross, 1)]], [])
        own_terms = [keep, over(other_keep, 1), over(cross_in, 2)]

        slots = [(2, [(near_mid, 0), (near_end, 0)], 0)]
        (gg,) = project(late, slots, gated_t, weight, gg, half, ("inner",), [cross_in], [2])
        own_in = add_blocks([own_terms], [gg])
        own_terms.append(over(own_in, 4))

        keeps, crosses = [], []
        for n, (offset, wide) in enumerate(pieces):
            slots = [
                (2, [(near_mid, offset // wide), (near_end, offset // wide)], offset),
                (3, [(far_mid[n], 0), (far_end[n], 0)], offset),
            ]
            if n == 0:
                gg, *outer = project(
                    late, slots, gated_t, weight, gg, wide, ("outer", "inner"), [own_in], [3]
                )
            else:
                earlier = [] if n == 1 else [gg, own_terms[-1]]
                outer = project(late, slots, gated_t, weight, None, wide, ("outer",), earlier, [], joined=True)
            if n == 0:
                keep, other_keep, cross, other_cross = outer
                keeps.append([keep, over(other_keep, 1)])
                crosses.append([cross, over(other_cross, 1)])
            else:
                keep, cross, other = outer
                got = over(other, 1)
                keeps.append([keep, (got, 0)])
                crosses.append([cross, (got, 1)])
            if n == 1:
                first_cross = add_blocks([crosses[0]], [keep], 0.1)
                keeps[0].append(over(first_cross, 2))
                (gg,) = project(
                    late, slots[1:], gated_t, weight, gg, wide, ("inner",), [first_cross], [3], 0.1
                )
        first_in = add_blocks([keeps[0]], [])
        last_cross = add_blocks(crosses[1:], [first_in])
        last_over = over(last_cross, 2)
        grad_query, grad_key, grad_value, first, last, even, odd = gradients(
            late, slots[1:], weight, wide, gg, conv, query, key, value, is_start, before, taps, consts,
            scale, [last_cross],
        )
        first_over = over(first_in, 4)
        grad_weight = finish(is_early, own_terms, keeps[:1], [first_over], None, 0, scale)
        last_in = add_blocks(keeps[1:], [first, first_over], 1, [last_over])
        last_over_y = over(last_in, 4)
        got = over(hold(odd, [last_in]), 1)
        grad_key, grad_value = complete(first, last, grad_key, grad_value)
        got = hold(got, [grad_weight, grad_key])
        others = [over(even[n] + got[n], 2 * n) for n in (1, 2, 3)]
        grad_weight = finish(
            is_early, own_terms, keeps[1:], [last_over, last_over_y], grad_weight, 1, scale
        )
        others[0] = hold(others[0], [grad_weight])
        grad_filter = even[0] + got[0] + sum(others)
    else:
        conv, gated_t = filtered(is_start, query, key, value, before, taps, consts)
        segment = lax.all_gather(out_grad, "tensor", axis=1, tiled=True)
        gg = lax.dot_general(segment, weight, (((1,), (1,)), ((), ())), preferred_element_type=F32)
        outer = dot(gated_t, segment)
        grad_weight = lax.psum_scatter(outer, "context", scatter_dimension=1, tiled=True) * scale
        grad_query, grad_key, grad_value, first, last, part = gradients(
            jnp.zeros((1,), jnp.int32), None, weight, 0, gg, conv, query, key, value, is_start, before, taps, consts,
            scale, [],
        )
        grad_filter = lax.psum_scatter(part, "context", scatter_dimension=1, tiled=True)
        grad_key, grad_value = complete(first, last, grad_key, grad_value)


    return (grad_query, grad_key, grad_value, grad_filter, grad_weight)


def solution(mesh):
    placed = (
        P("context", "tensor"),
        P("context", "tensor"),
        P("context", "tensor"),
        P(None, "tensor"),
        P("tensor", None),
        P("context", "tensor"),
    )
    run = functools.partial(body, tensors=mesh.shape["tensor"], contexts=mesh.shape["context"])
    return jax.shard_map(
        run,
        mesh=mesh,
        in_specs=placed,
        out_specs=(
            P("context", "tensor"),
            P("context", "tensor"),
            P("context", "tensor"),
            P(None, ("tensor", "context")),
            P("tensor", "context"),
        ),
        check_vma=False,
    )
```
